32 devices in a mesh: tm: 4 (over y, x), map: 8 (over z, core).
Axes of the slice: x: 2, y: 2, z: 4, core: 2. Of those that a mesh axis runs over, the one named last changes fastest.
Arguments:
- tiles: float32 [4, 2, 64, 4, 128, 128], P('tm', None, 'map'), may hold values from -0.25 to 0.25
- columns: int32 [4, 2, 64, 4], P('tm', None, 'map'), may hold values from 0 to 63, as said below
- window_steps: int32 [4], P('tm'), may hold values from 1 to 2
- direction: float32 [8, 64, 128], P(None, 'map'), may hold values from -6 to 6
- forcing: float32 [4, 2, 64, 128], P('tm', None, 'map'), may hold values from 0.05 to 0.5
- observe: float32 [4, 2, 64, 128], P('tm', None, 'map'), may hold values from 0.1 to 1
Outputs:
- hessian_action: float32 [8, 64, 128], P('tm', 'map')
The draws below stay inside these ranges and needn't reach their ends.
Inputs may be any that keep to these rules, and one draw needn't show every extreme that they name: `columns`: every column index of block row r lies between p * 8 - 2 and (p + 1) * 8 + 1, where p = r // 8.
All inputs are finite; a program needn't handle non-finite values.
Results may differ from the reference program's by a relative error of at most 0.0001.
Values sent between devices are 32-bit elements; how exact they have to be, the bound alone decides.
A program may use at most 64 MiB of HBM per device.

```python
import math
import jax
import jax.numpy as jnp
from jax import lax

TILE = 128
NNZ = 4
HALO = 2
K = 2
DIRS = 8
NBD = 8
NWIN = 4
NB = 64


def draw_columns(key, part):
    offsets = jax.random.randint(key, (NWIN, K, NB, NNZ), -HALO, NBD + HALO)
    row_ids = jnp.arange(NB, dtype=jnp.int32)
    partition = row_ids // NBD
    local_row = row_ids % NBD
    slot_ids = jnp.arange(NNZ, dtype=jnp.int32)
    lowest = (local_row[:, None] == 0) & (slot_ids[None, :] == 0)
    highest = (local_row[:, None] == NBD - 1) & (slot_ids[None, :] == 0)
    offsets = jnp.where(lowest[None, None], -HALO, offsets)
    offsets = jnp.where(highest[None, None], NBD + HALO - 1, offsets)
    result = partition[None, None, :, None] * NBD + offsets
    return jnp.clip(result, 0, NB - 1).astype(jnp.int32)


def draw_window_steps(key, part):
    counts = jax.random.randint(key, (NWIN,), 1, K + 1)
    position = jax.random.randint(jax.random.fold_in(key, 7), (), 0, NWIN)
    counts = jnp.where(jnp.arange(NWIN) == position, K, counts)
    return counts.astype(jnp.int32)


def levels(rng, dims, cuts, least, high):
    loudness = 1.0
    for axis_at, parts in cuts:
        draws = jax.random.uniform(jax.random.fold_in(jax.random.fold_in(rng, 6), axis_at), (parts,), jnp.float32, least / len(cuts), high / len(cuts))
        loudness = loudness * jnp.repeat(jnp.exp(draws), dims[axis_at] // parts).reshape((-1,) + (1,) * (len(dims) - 1 - axis_at))
    return loudness


def scatter_about(rng, extent, width, most, split=(), kind=jnp.bfloat16):
    level = levels(rng, extent, split, -0.22, 0.18) if split else 1.0
    array = jax.random.normal(rng, extent, jnp.float32) * width * level
    return jnp.minimum(jnp.maximum(array, -most), most).astype(kind)


def setup_inputs(seed: int = 0) -> dict:
    key_list = jax.random.split(jax.random.key(seed), 7)
    return {
        "tiles": scatter_about(key_list[0], (NWIN, K, NB, NNZ, TILE, TILE), (NNZ * TILE * 17 // 16) ** -0.5, 0.25, ((0, 4), (2, 8)), jnp.float32),
        "columns": draw_columns(jax.random.fold_in(key_list[6], 71), 0),
        "window_steps": draw_window_steps(jax.random.fold_in(key_list[6], 71), 0),
        "direction": scatter_about(key_list[3], (DIRS, NB, TILE), 1.0, 6.0, ((1, 8),), jnp.float32),
        "forcing": jnp.clip(jnp.exp(math.log(0.5) - 2.3025851 * jax.random.uniform(key_list[4], (NWIN, K, NB, TILE), jnp.float32) ** levels(key_list[4], (NWIN, K, NB, TILE), ((0, 4), (2, 8)), -0.2, 0.2)), 0.05, 0.5),
        "observe": jnp.clip(jnp.exp(math.log(1.0) - 2.3025851 * jax.random.uniform(key_list[5], (NWIN, K, NB, TILE), jnp.float32) ** levels(key_list[5], (NWIN, K, NB, TILE), ((0, 4), (2, 8)), -0.2, 0.2)), 0.1, 1.0),
    }


def reference(tiles, columns, window_steps, direction, forcing, observe):
    window_count = tiles.shape[0]
    step_count = tiles.shape[1]
    current = jnp.zeros(direction.shape, jnp.float32)
    history = []
    for window in range(window_count):
        window_states = [current]
        for step_index in range(step_count):
            column_ids = columns[window, step_index].reshape(-1)
            picked = jnp.take(current, column_ids, axis=1).reshape(DIRS, NB, NNZ, TILE)
            product = jnp.einsum("dbje,bjce->dbc", picked, tiles[window, step_index], precision=lax.Precision.HIGHEST)
            updated = product + forcing[window, step_index][None] * direction
            current = jnp.where(step_index < window_steps[window], updated, current)
            window_states.append(current)
        history.append(window_states)
    carried = jnp.zeros(direction.shape, jnp.float32)
    gradient = jnp.zeros(direction.shape, jnp.float32)
    for window in range(window_count - 1, -1, -1):
        for step_index in range(step_count - 1, -1, -1):
            active = step_index < window_steps[window]
            adjoint = carried + observe[window, step_index][None] * history[window][step_index + 1]
            gradient = gradient + jnp.where(active, forcing[window, step_index][None] * adjoint, 0.0)
            contrib = jnp.einsum("dbc,bjce->dbje", adjoint, tiles[window, step_index], precision=lax.Precision.HIGHEST)
            contrib = contrib.reshape(DIRS, NB * NNZ, TILE)
            column_ids = columns[window, step_index].reshape(-1)
            spread = jax.ops.segment_sum(jnp.moveaxis(contrib, 1, 0), column_ids, num_segments=NB)
            spread = jnp.moveaxis(spread, 0, 1)
            carried = jnp.where(active, spread, carried)
    return gradient
```

```python
import functools

import jax
import jax.numpy as jnp
from jax import lax
from jax.experimental import pallas as pl
from jax.experimental.pallas import tpu as pltpu
from jax.sharding import PartitionSpec as P

HALO = 2
MESH = pl.DeviceIdType.MESH
F32 = jnp.float32
BF16 = jnp.bfloat16


def split(x):
    high = x.astype(BF16).astype(F32)
    return jnp.concatenate([high, x - high], axis=0).astype(BF16)


def kernel(
    windows,
    parts,
    tiles,
    columns,
    steps,
    direction,
    forcing,
    observe,
    out,
    raw,
    weights,
    ext0,
    ext1,
    state1,
    state2,
    fin,
    fhalo,
    bin_core,
    bin_rim,
    bhalo,
    brim_out,
    bcore_out,
    brim_out0,
    grad_out,
    grad_in,
    load_sem,
    fwd_send,
    fwd_recv,
    fh_send,
    fh_recv,
    bwd_send,
    bwd_recv,
    bh_send,
    bh_recv,
    g_send,
    g_recv,
):
    dirs, nb, tile = direction.shape
    slots = columns.shape[3]
    width = nb + 2 * HALO
    dpw = dirs // windows
    w = lax.axis_index("tm")
    p = lax.axis_index("map")
    has_prev, has_next = w > 0, w < windows - 1
    has_lo, has_hi = p > 0, p < parts - 1

    loads = [
        pltpu.make_async_copy(tiles.at[0, k], raw.at[k], load_sem.at[k]) for k in range(2)
    ]
    for load in loads:
        load.start()
    for ref in (fin, fhalo, bin_core, bin_rim, bhalo):
        ref[...] = jnp.zeros(ref.shape, F32)

    barrier = pltpu.get_barrier_semaphore()
    count = jnp.int32(0)
    for dw in (-1, 0, 1):
        for dp in (-1, 0, 1):
            if dp == 0:
                continue
            ok = (w + dw >= 0) & (w + dw < windows) & (p + dp >= 0) & (p + dp < parts)

            @pl.when(ok)
            def _():
                pl.semaphore_signal(
                    barrier, inc=1, device_id={"tm": w + dw, "map": p + dp}, device_id_type=MESH
                )

            count = count + ok.astype(jnp.int32)
    for o in range(1, windows):
        pl.semaphore_signal(
            barrier, inc=1, device_id={"tm": lax.rem(w + o, windows)}, device_id_type=MESH
        )
    count = count + (windows - 1)

    first = p * nb - HALO
    local = [
        [
            [jnp.clip(columns[0, k, b, j] - first, 0, width - 1) for j in range(slots)]
            for b in range(nb)
        ]
        for k in range(2)
    ]
    active = [jnp.full((dirs, tile), steps[0], jnp.int32) > k for k in range(2)]

    def convert(k):
        def row(b, carry):
            for j in range(slots):
                x = raw[k, b, j]
                high = x.astype(BF16)
                weights[k, b, :tile, j * tile : (j + 1) * tile] = high
                weights[k, b, tile:, j * tile : (j + 1) * tile] = (
                    x - high.astype(F32)
                ).astype(BF16)
            return carry

        lax.fori_loop(0, nb, row, 0)

    pending = []

    def send(ok, src, dst, send_sem, recv_sem, target):
        copy = pltpu.make_async_remote_copy(
            src_ref=src,
            dst_ref=dst,
            send_sem=send_sem,
            recv_sem=recv_sem,
            device_id=target,
            device_id_type=MESH,
        )

        @pl.when(ok)
        def _():
            copy.start()

        pending.append((ok, copy))

    def arrived(ok, dst, send_sem, recv_sem):
        copy = pltpu.make_async_remote_copy(
            src_ref=dst,
            dst_ref=dst,
            send_sem=send_sem,
            recv_sem=recv_sem,
            device_id={"tm": w, "map": p},
            device_id_type=MESH,
        )

        @pl.when(ok)
        def _():
            copy.wait_recv()

    chunks = ((0, HALO), (nb - HALO, HALO), (HALO, nb - 2 * HALO))
    order = [*range(HALO), *range(nb - HALO, nb), *range(HALO, nb - HALO)]
    low, high_at = slice(0, HALO), slice(HALO, 2 * HALO)

    load_rows = [direction[:, b, :] for b in range(nb)]
    loads[0].wait()
    convert(0)
    loads[1].wait()
    convert(1)

    def product(k, ext, b):
        lhs = jnp.concatenate([ext[local[k][b][j]] for j in range(slots)], axis=1)
        r = lax.dot_general(
            lhs, weights[k, b], (((1,), (1,)), ((), ())), preferred_element_type=F32
        )
        r = r[:dirs] + r[dirs:]
        return r[:, :tile] + r[:, tile:]

    for i, (start, size) in enumerate(chunks):
        arrived(has_prev, fin.at[pl.ds(HALO + start, size)], fwd_send.at[i], fwd_recv.at[i])
    arrived(has_prev & has_lo, fin.at[pl.ds(0, HALO)], fwd_send.at[3], fwd_recv.at[3])
    arrived(
        has_prev & has_hi, fin.at[pl.ds(HALO + nb, HALO)], fwd_send.at[4], fwd_recv.at[4]
    )
    for q in range(width):
        ext0[q] = split(fin[q])
    for n, b in enumerate(order):
        new = product(0, ext0, b) + forcing[0, 0, b : b + 1] * load_rows[b]
        new = jnp.where(active[0], new, fin[HALO + b])
        state1[b] = new
        ext1[HALO + b] = split(new)
        if n == 2 * HALO - 1:
            pl.semaphore_wait(barrier, count)
            send(
                has_lo,
                state1.at[pl.ds(0, HALO)],
                fhalo.at[high_at],
                fh_send.at[0],
                fh_recv.at[0],
                {"tm": w, "map": p - 1},
            )
            send(
                has_hi,
                state1.at[pl.ds(nb - HALO, HALO)],
                fhalo.at[low],
                fh_send.at[1],
                fh_recv.at[1],
                {"tm": w, "map": p + 1},
            )
    arrived(has_hi, fhalo.at[high_at], fh_send.at[0], fh_recv.at[0])
    arrived(has_lo, fhalo.at[low], fh_send.at[1], fh_recv.at[1])
    for q in range(HALO):
        ext1[q] = split(fhalo[q])
        ext1[HALO + nb + q] = split(fhalo[HALO + q])
    for n, b in enumerate(order):
        new = product(1, ext1, b) + forcing[0, 1, b : b + 1] * load_rows[b]
        state2[b] = jnp.where(active[1], new, state1[b])
        if n == HALO - 1:
            send(
                has_next & has_lo,
                state2.at[pl.ds(0, HALO)],
                fin.at[pl.ds(HALO + nb, HALO)],
                fwd_send.at[4],
                fwd_recv.at[4],
                {"tm": w + 1, "map": p - 1},
            )
        if n == 2 * HALO - 1:
            send(
                has_next & has_hi,
                state2.at[pl.ds(nb - HALO, HALO)],
                fin.at[pl.ds(0, HALO)],
                fwd_send.at[3],
                fwd_recv.at[3],
                {"tm": w + 1, "map": p + 1},
            )
        for i, (start, size) in enumerate(chunks):
            if n == (HALO - 1, 2 * HALO - 1, nb - 1)[i]:
                send(
                    has_next,
                    state2.at[pl.ds(start, size)],
                    fin.at[pl.ds(HALO + start, size)],
                    fwd_send.at[i],
                    fwd_recv.at[i],
                    {"tm": w + 1, "map": p},
                )

    def scatter(k, b, a, spread):
        s = split(a)
        r = lax.dot_general(
            jnp.concatenate([s, s], axis=1),
            weights[k, b],
            (((1,), (0,)), ((), ())),
            preferred_element_type=F32,
        )
        r = r[:dirs] + r[dirs:]
        for j in range(slots):
            at = jnp.full((dirs, tile), local[k][b][j], jnp.int32)
            part = r[:, j * tile : (j + 1) * tile]
            for q in range(width):
                spread[q] = spread[q] + jnp.where(at == q, part, 0.0)

    seen1 = [observe[0, 1, b : b + 1] * state2[b] for b in range(nb)]
    arrived(has_next, bin_core, bwd_send.at[0], bwd_recv.at[0])
    arrived(has_next & has_lo, bin_rim.at[low], bwd_send.at[1], bwd_recv.at[1])
    arrived(has_next & has_hi, bin_rim.at[high_at], bwd_send.at[2], bwd_recv.at[2])
    carried = [bin_core[b] for b in range(nb)]
    for q in range(HALO):
        carried[q] = carried[q] + bin_rim[q]
        carried[nb - HALO + q] = carried[nb - HALO + q] + bin_rim[HALO + q]
    zero = jnp.zeros((dirs, tile), F32)
    spread = [zero] * width
    gradient = [None] * nb
    for b in range(nb):
        a = carried[b] + seen1[b]
        gradient[b] = jnp.where(active[1], forcing[0, 1, b : b + 1] * a, 0.0)
        scatter(1, b, a, spread)
    for q in range(HALO):
        brim_out[q] = spread[q]
        brim_out[HALO + q] = spread[HALO + nb + q]
    send(
        has_lo,
        brim_out.at[low],
        bhalo.at[high_at],
        bh_send.at[0],
        bh_recv.at[0],
        {"tm": w, "map": p - 1},
    )
    send(
        has_hi,
        brim_out.at[high_at],
        bhalo.at[low],
        bh_send.at[1],
        bh_recv.at[1],
        {"tm": w, "map": p + 1},
    )
    inner = spread[HALO : HALO + nb]
    spread = [zero] * width
    after1 = list(carried)
    for n, b in enumerate([*range(HALO, nb - HALO), *range(HALO), *range(nb - HALO, nb)]):
        if n == nb - 2 * HALO:
            arrived(has_hi, bhalo.at[high_at], bh_send.at[0], bh_recv.at[0])
            arrived(has_lo, bhalo.at[low], bh_send.at[1], bh_recv.at[1])
        value = inner[b]
        if b < HALO:
            value = value + bhalo[b]
        if b >= nb - HALO:
            value = value + bhalo[HALO + b - (nb - HALO)]
        value = jnp.where(active[1], value, carried[b])
        after1[b] = value
        a = value + observe[0, 0, b : b + 1] * state1[b]
        gradient[b] = gradient[b] + jnp.where(
            active[0], forcing[0, 0, b : b + 1] * a, 0.0
        )
        scatter(0, b, a, spread)
    for q in range(HALO):
        brim_out0[q] = jnp.where(active[0], spread[q], 0.0)
        brim_out0[HALO + q] = jnp.where(active[0], spread[HALO + nb + q], 0.0)
    for b in range(nb):
        bcore_out[b] = jnp.where(active[0], spread[HALO + b], after1[b])
    send(
        has_prev & has_lo,
        brim_out0.at[low],
        bin_rim.at[high_at],
        bwd_send.at[2],
        bwd_recv.at[2],
        {"tm": w - 1, "map": p - 1},
    )
    send(
        has_prev & has_hi,
        brim_out0.at[high_at],
        bin_rim.at[low],
        bwd_send.at[1],
        bwd_recv.at[1],
        {"tm": w - 1, "map": p + 1},
    )
    send(
        has_prev,
        bcore_out,
        bin_core,
        bwd_send.at[0],
        bwd_recv.at[0],
        {"tm": w - 1, "map": p},
    )

    for b in range(nb):
        grad_out[:, b, :] = gradient[b]
    always = w >= 0
    for o in range(1, windows):
        target = lax.rem(w + o, windows)
        send(
            always,
            grad_out.at[pl.ds(target * dpw, dpw)],
            grad_in.at[o - 1],
            g_send.at[o - 1],
            g_recv.at[o - 1],
            {"tm": target, "map": p},
        )
    total = grad_out[pl.ds(w * dpw, dpw)]
    for o in range(1, windows):
        arrived(always, grad_in.at[o - 1], g_send.at[o - 1], g_recv.at[o - 1])
        total = total + grad_in[o - 1]
    out[...] = total
    for ok, copy in pending:

        @pl.when(ok)
        def _():
            copy.wait_send()


def shards(windows, parts, tiles, columns, window_steps, direction, forcing, observe):
    dirs, nb, tile = direction.shape
    slots = tiles.shape[3]
    width = nb + 2 * HALO
    dpw = dirs // windows
    vmem = pl.BlockSpec(memory_space=pltpu.VMEM)
    smem = pl.BlockSpec(memory_space=pltpu.SMEM)
    block = lambda *lead: pltpu.VMEM((*lead, dirs, tile), F32)
    sems = lambda n: pltpu.SemaphoreType.DMA((n,))
    return pl.pallas_call(
        functools.partial(kernel, windows, parts),
        out_shape=jax.ShapeDtypeStruct((dpw, nb, tile), F32),
        in_specs=[pl.BlockSpec(memory_space=pl.ANY), smem, smem, vmem, vmem, vmem],
        out_specs=vmem,
        scratch_shapes=[
            pltpu.VMEM((2, nb, slots, tile, tile), F32),
            pltpu.VMEM((2, nb, 2 * tile, slots * tile), BF16),
            pltpu.VMEM((width, 2 * dirs, tile), BF16),
            pltpu.VMEM((width, 2 * dirs, tile), BF16),
            block(nb),
            block(nb),
            block(width),
            block(2 * HALO),
            block(nb),
            block(2 * HALO),
            block(2 * HALO),
            block(2 * HALO),
            block(nb),
            block(2 * HALO),
            pltpu.VMEM((dirs, nb, tile), F32),
            pltpu.VMEM((windows - 1, dpw, nb, tile), F32),
            sems(2),
            sems(5),
            sems(5),
            sems(2),
            sems(2),
            sems(3),
            sems(3),
            sems(2),
            sems(2),
            sems(windows - 1),
            sems(windows - 1),
        ],
        compiler_params=pltpu.CompilerParams(
            collective_id=0, has_side_effects=True, vmem_limit_bytes=32 * 1024 * 1024
        ),
    )(tiles, columns, window_steps, direction, forcing, observe)


def solution(mesh):
    placed = (
        P("tm", None, "map", None, None, None),
        P("tm", None, "map", None),
        P("tm"),
        P(None, "map", None),
        P("tm", None, "map", None),
        P("tm", None, "map", None),
    )
    return jax.shard_map(
        functools.partial(shards, mesh.shape["tm"], mesh.shape["map"]),
        mesh=mesh,
        in_specs=placed,
        out_specs=P("tm", "map", None),
        check_vma=False,
    )
```

```python
import functools

import jax
import jax.numpy as jnp
from jax import lax
from jax.experimental import pallas as pl
from jax.experimental.pallas import tpu as pltpu
from jax.sharding import PartitionSpec as P

HALO = 2
MESH = pl.DeviceIdType.MESH
F32 = jnp.float32
BF16 = jnp.bfloat16


def split(x):
    high = x.astype(BF16).astype(F32)
    return jnp.concatenate([high, x - high], axis=0).astype(BF16)


def kernel(
    windows,
    parts,
    tiles,
    columns,
    steps,
    direction_far,
    forcing_far,
    observe_far,
    out,
    direction,
    forcing,
    observe,
    raw,
    weights,
    ext0,
    ext1,
    state1,
    state2,
    fin,
    fhalo,
    bin_core,
    bin_rim,
    bhalo,
    brim_out,
    bcore_out,
    brim_out0,
    grad_out,
    grad_in,
    small_sem,
    load_sem,
    fwd_send,
    fwd_recv,
    fh_send,
    fh_recv,
    bwd_send,
    bwd_recv,
    bh_send,
    bh_recv,
    g_send,
    g_recv,
):
    dirs, nb, tile = direction.shape
    slots = columns.shape[2]
    width = nb + 2 * HALO
    dpw = dirs // windows
    w = lax.axis_index("tm")
    p = lax.axis_index("map")
    has_prev, has_next = w > 0, w < windows - 1
    has_lo, has_hi = p > 0, p < parts - 1

    def load(k, b):
        return pltpu.make_async_copy(tiles.at[0, k, b], raw.at[k, b], load_sem.at[k, b])

    for b in range(nb):
        load(0, b).start()
    small = [
        pltpu.make_async_copy(src, dst, small_sem.at[i])
        for i, (src, dst) in enumerate(
            ((direction_far, direction), (forcing_far, forcing), (observe_far, observe))
        )
    ]
    for copy in small:
        copy.start()
    for b in range(nb):
        load(1, b).start()
    for ref in (fin, fhalo, bin_core, bin_rim, bhalo):
        ref[...] = jnp.zeros(ref.shape, F32)

    barrier = pltpu.get_barrier_semaphore()
    count = jnp.int32(0)
    for dw in (-1, 0, 1):
        for dp in (-1, 0, 1):
            if dp == 0:
                continue
            ok = (w + dw >= 0) & (w + dw < windows) & (p + dp >= 0) & (p + dp < parts)

            @pl.when(ok)
            def _():
                pl.semaphore_signal(
                    barrier, inc=1, device_id={"tm": w + dw, "map": p + dp}, device_id_type=MESH
                )

            count = count + ok.astype(jnp.int32)
    for o in range(1, windows):
        pl.semaphore_signal(
            barrier, inc=1, device_id={"tm": lax.rem(w + o, windows)}, device_id_type=MESH
        )
    count = count + (windows - 1)

    first = p * nb - HALO
    local = [
        [
            [jnp.clip(columns[0, k, j, b] - first, 0, width - 1) for j in range(slots)]
            for b in range(nb)
        ]
        for k in range(2)
    ]
    active = [jnp.full((dirs, tile), steps[0], jnp.int32) > k for k in range(2)]

    def convert(k):
        def row(b, carry):
            load(k, b).wait()
            for j in range(slots):
                x = raw[k, b, j]
                high = x.astype(BF16)
                weights[k, b, :tile, j * tile : (j + 1) * tile] = high
                weights[k, b, tile:, j * tile : (j + 1) * tile] = (
                    x - high.astype(F32)
                ).astype(BF16)
            return carry

        lax.fori_loop(0, nb, row, 0)

    pending = []

    def send(ok, src, dst, send_sem, recv_sem, target):
        copy = pltpu.make_async_remote_copy(
            src_ref=src,
            dst_ref=dst,
            send_sem=send_sem,
            recv_sem=recv_sem,
            device_id=target,
            device_id_type=MESH,
        )

        @pl.when(ok)
        def _():
            copy.start()

        pending.append((ok, copy))

    def arrived(ok, dst, send_sem, recv_sem):
        copy = pltpu.make_async_remote_copy(
            src_ref=dst,
            dst_ref=dst,
            send_sem=send_sem,
            recv_sem=recv_sem,
            device_id={"tm": w, "map": p},
            device_id_type=MESH,
        )

        @pl.when(ok)
        def _():
            copy.wait_recv()

    chunks = ((0, HALO), (nb - HALO, HALO), (HALO, nb - 2 * HALO))
    order = [*range(HALO), *range(nb - HALO, nb), *range(HALO, nb - HALO)]
    low, high_at = slice(0, HALO), slice(HALO, 2 * HALO)

    convert(0)

    @pl.when(has_prev)
    def _():
        convert(1)

    for copy in small:
        copy.wait()
    load_rows = [direction[:, b, :] for b in range(nb)]

    def product(k, ext, b):
        lhs = jnp.concatenate([ext[local[k][b][j]] for j in range(slots)], axis=1)
        r = lax.dot_general(
            lhs, weights[k, b], (((1,), (1,)), ((), ())), preferred_element_type=F32
        )
        r = r[:dirs] + r[dirs:]
        return r[:, :tile] + r[:, tile:]

    for i, (start, size) in enumerate(chunks):
        arrived(has_prev, fin.at[pl.ds(HALO + start, size)], fwd_send.at[i], fwd_recv.at[i])
    arrived(has_prev & has_lo, fin.at[pl.ds(0, HALO)], fwd_send.at[3], fwd_recv.at[3])
    arrived(
        has_prev & has_hi, fin.at[pl.ds(HALO + nb, HALO)], fwd_send.at[4], fwd_recv.at[4]
    )
    for q in range(width):
        ext0[q] = split(fin[q])
    for n, b in enumerate(order):
        new = product(0, ext0, b) + forcing[0, 0, b : b + 1] * load_rows[b]
        new = jnp.where(active[0], new, fin[HALO + b])
        state1[b] = new
        ext1[HALO + b] = split(new)
        if n == 2 * HALO - 1:
            pl.semaphore_wait(barrier, count)
            send(
                has_lo,
                state1.at[pl.ds(0, HALO)],
                fhalo.at[high_at],
                fh_send.at[0],
                fh_recv.at[0],
                {"tm": w, "map": p - 1},
            )
            send(
                has_hi,
                state1.at[pl.ds(nb - HALO, HALO)],
                fhalo.at[low],
                fh_send.at[1],
                fh_recv.at[1],
                {"tm": w, "map": p + 1},
            )

    @pl.when(w == 0)
    def _():
        convert(1)

    arrived(has_hi, fhalo.at[high_at], fh_send.at[0], fh_recv.at[0])
    arrived(has_lo, fhalo.at[low], fh_send.at[1], fh_recv.at[1])
    for q in range(HALO):
        ext1[q] = split(fhalo[q])
        ext1[HALO + nb + q] = split(fhalo[HALO + q])
    for n, b in enumerate(order):
        new = product(1, ext1, b) + forcing[0, 1, b : b + 1] * load_rows[b]
        state2[b] = jnp.where(active[1], new, state1[b])
        if n == HALO - 1:
            send(
                has_next & has_lo,
                state2.at[pl.ds(0, HALO)],
                fin.at[pl.ds(HALO + nb, HALO)],
                fwd_send.at[4],
                fwd_recv.at[4],
                {"tm": w + 1, "map": p - 1},
            )
        if n == 2 * HALO - 1:
            send(
                has_next & has_hi,
                state2.at[pl.ds(nb - HALO, HALO)],
                fin.at[pl.ds(0, HALO)],
                fwd_send.at[3],
                fwd_recv.at[3],
                {"tm": w + 1, "map": p + 1},
            )
        for i, (start, size) in enumerate(chunks):
            if n == (HALO - 1, 2 * HALO - 1, nb - 1)[i]:
                send(
                    has_next,
                    state2.at[pl.ds(start, size)],
                    fin.at[pl.ds(HALO + start, size)],
                    fwd_send.at[i],
                    fwd_recv.at[i],
                    {"tm": w + 1, "map": p},
                )

    def scatter(k, b, a, spread):
        s = split(a)
        r = lax.dot_general(
            jnp.concatenate([s, s], axis=1),
            weights[k, b],
            (((1,), (0,)), ((), ())),
            preferred_element_type=F32,
        )
        r = r[:dirs] + r[dirs:]
        for j in range(slots):
            at = jnp.full((dirs, tile), local[k][b][j], jnp.int32)
            part = r[:, j * tile : (j + 1) * tile]
            for q in range(width):
                spread[q] = spread[q] + jnp.where(at == q, part, 0.0)

    seen1 = [observe[0, 1, b : b + 1] * state2[b] for b in range(nb)]
    arrived(has_next, bin_core, bwd_send.at[0], bwd_recv.at[0])
    arrived(has_next & has_lo, bin_rim.at[low], bwd_send.at[1], bwd_recv.at[1])
    arrived(has_next & has_hi, bin_rim.at[high_at], bwd_send.at[2], bwd_recv.at[2])
    carried = [bin_core[b] for b in range(nb)]
    for q in range(HALO):
        carried[q] = carried[q] + bin_rim[q]
        carried[nb - HALO + q] = carried[nb - HALO + q] + bin_rim[HALO + q]
    zero = jnp.zeros((dirs, tile), F32)
    spread = [zero] * width
    gradient = [None] * nb
    for b in range(nb):
        a = carried[b] + seen1[b]
        gradient[b] = jnp.where(active[1], forcing[0, 1, b : b + 1] * a, 0.0)
        scatter(1, b, a, spread)
    for q in range(HALO):
        brim_out[q] = spread[q]
        brim_out[HALO + q] = spread[HALO + nb + q]
    send(
        has_lo,
        brim_out.at[low],
        bhalo.at[high_at],
        bh_send.at[0],
        bh_recv.at[0],
        {"tm": w, "map": p - 1},
    )
    send(
        has_hi,
        brim_out.at[high_at],
        bhalo.at[low],
        bh_send.at[1],
        bh_recv.at[1],
        {"tm": w, "map": p + 1},
    )
    inner = spread[HALO : HALO + nb]
    spread = [zero] * width
    after1 = list(carried)
    for n, b in enumerate([*range(HALO, nb - HALO), *range(HALO), *range(nb - HALO, nb)]):
        if n == nb - 2 * HALO:
            arrived(has_hi, bhalo.at[high_at], bh_send.at[0], bh_recv.at[0])
            arrived(has_lo, bhalo.at[low], bh_send.at[1], bh_recv.at[1])
        value = inner[b]
        if b < HALO:
            value = value + bhalo[b]
        if b >= nb - HALO:
            value = value + bhalo[HALO + b - (nb - HALO)]
        value = jnp.where(active[1], value, carried[b])
        after1[b] = value
        a = value + observe[0, 0, b : b + 1] * state1[b]
        gradient[b] = gradient[b] + jnp.where(
            active[0], forcing[0, 0, b : b + 1] * a, 0.0
        )
        scatter(0, b, a, spread)
    for q in range(HALO):
        brim_out0[q] = jnp.where(active[0], spread[q], 0.0)
        brim_out0[HALO + q] = jnp.where(active[0], spread[HALO + nb + q], 0.0)
    for b in range(nb):
        bcore_out[b] = jnp.where(active[0], spread[HALO + b], after1[b])
    send(
        has_prev & has_lo,
        brim_out0.at[low],
        bin_rim.at[high_at],
        bwd_send.at[2],
        bwd_recv.at[2],
        {"tm": w - 1, "map": p - 1},
    )
    send(
        has_prev & has_hi,
        brim_out0.at[high_at],
        bin_rim.at[low],
        bwd_send.at[1],
        bwd_recv.at[1],
        {"tm": w - 1, "map": p + 1},
    )
    send(
        has_prev,
        bcore_out,
        bin_core,
        bwd_send.at[0],
        bwd_recv.at[0],
        {"tm": w - 1, "map": p},
    )

    for b in range(nb):
        grad_out[:, b, :] = gradient[b]
    always = w >= 0
    for o in range(1, windows):
        target = lax.rem(w + o, windows)
        send(
            always,
            grad_out.at[pl.ds(target * dpw, dpw)],
            grad_in.at[o - 1],
            g_send.at[o - 1],
            g_recv.at[o - 1],
            {"tm": target, "map": p},
        )
    total = grad_out[pl.ds(w * dpw, dpw)]
    for o in range(1, windows):
        arrived(always, grad_in.at[o - 1], g_send.at[o - 1], g_recv.at[o - 1])
        total = total + grad_in[o - 1]
    out[...] = total
    for ok, copy in pending:

        @pl.when(ok)
        def _():
            copy.wait_send()


def shards(windows, parts, tiles, columns, window_steps, direction, forcing, observe):
    dirs, nb, tile = direction.shape
    slots = tiles.shape[3]
    width = nb + 2 * HALO
    dpw = dirs // windows
    vmem = pl.BlockSpec(memory_space=pltpu.VMEM)
    hbm = pl.BlockSpec(memory_space=pltpu.HBM)
    smem = pl.BlockSpec(memory_space=pltpu.SMEM)
    block = lambda *lead: pltpu.VMEM((*lead, dirs, tile), F32)
    sems = lambda n: pltpu.SemaphoreType.DMA((n,))
    return pl.pallas_call(
        functools.partial(kernel, windows, parts),
        out_shape=jax.ShapeDtypeStruct((dpw, nb, tile), F32),
        in_specs=[hbm, smem, smem, hbm, hbm, hbm],
        out_specs=vmem,
        scratch_shapes=[
            pltpu.VMEM(direction.shape, F32),
            pltpu.VMEM(forcing.shape, F32),
            pltpu.VMEM(observe.shape, F32),
            pltpu.VMEM((2, nb, slots, tile, tile), F32),
            pltpu.VMEM((2, nb, 2 * tile, slots * tile), BF16),
            pltpu.VMEM((width, 2 * dirs, tile), BF16),
            pltpu.VMEM((width, 2 * dirs, tile), BF16),
            block(nb),
            block(nb),
            block(width),
            block(2 * HALO),
            block(nb),
            block(2 * HALO),
            block(2 * HALO),
            block(2 * HALO),
            block(nb),
            block(2 * HALO),
            pltpu.VMEM((dirs, nb, tile), F32),
            pltpu.VMEM((windows - 1, dpw, nb, tile), F32),
            sems(3),
            pltpu.SemaphoreType.DMA((2, nb)),
            sems(5),
            sems(5),
            sems(2),
            sems(2),
            sems(3),
            sems(3),
            sems(2),
            sems(2),
            sems(windows - 1),
            sems(windows - 1),
        ],
        compiler_params=pltpu.CompilerParams(
            collective_id=0, has_side_effects=True, vmem_limit_bytes=63 * 1024 * 1024
        ),
    )(tiles, jnp.swapaxes(columns, 2, 3), window_steps, direction, forcing, observe)


def solution(mesh):
    placed = (
        P("tm", None, "map", None, None, None),
        P("tm", None, "map", None),
        P("tm"),
        P(None, "map", None),
        P("tm", None, "map", None),
        P("tm", None, "map", None),
    )
    return jax.shard_map(
        functools.partial(shards, mesh.shape["tm"], mesh.shape["map"]),
        mesh=mesh,
        in_specs=placed,
        out_specs=P("tm", "map", None),
        check_vma=False,
    )
```

```python
import functools

import jax
import jax.numpy as jnp
from jax import lax
from jax.experimental import pallas as pl
from jax.experimental.pallas import tpu as pltpu
from jax.sharding import PartitionSpec as P

HALO = 2
MESH = pl.DeviceIdType.MESH
F32 = jnp.float32
BF16 = jnp.bfloat16


def split(x):
    high = x.astype(BF16).astype(F32)
    return jnp.concatenate([high, x - high], axis=0).astype(BF16)


def kernel(
    windows,
    parts,
    tiles,
    columns,
    steps,
    direction_far,
    forcing_far,
    observe_far,
    out,
    direction,
    forcing,
    observe,
    raw,
    weights,
    turned,
    made,
    ext0,
    ext1,
    state1,
    state2,
    fin,
    fhalo,
    bin_core,
    bin_rim,
    bhalo,
    brim_out,
    bcore_out,
    brim_out0,
    grad_out,
    grad_in,
    small_sem,
    load_sem,
    fwd_send,
    fwd_recv,
    fh_send,
    fh_recv,
    bwd_send,
    bwd_recv,
    bh_send,
    bh_recv,
    g_send,
    g_recv,
):
    dirs, nb, tile = direction.shape
    slots = columns.shape[2]
    width = nb + 2 * HALO
    dpw = dirs // windows
    w = lax.axis_index("tm")
    p = lax.axis_index("map")
    has_prev, has_next = w > 0, w < windows - 1
    has_lo, has_hi = p > 0, p < parts - 1

    def load(k, b):
        return pltpu.make_async_copy(tiles.at[0, k, b], raw.at[k, b], load_sem.at[k, b])

    for b in range(nb):
        load(0, b).start()
    small = [
        pltpu.make_async_copy(src, dst, small_sem.at[i])
        for i, (src, dst) in enumerate(
            ((direction_far, direction), (forcing_far, forcing), (observe_far, observe))
        )
    ]
    for copy in small:
        copy.start()
    for b in range(nb):
        load(1, b).start()
    for ref in (fin, fhalo, bin_core, bin_rim, bhalo):
        ref[...] = jnp.zeros(ref.shape, F32)

    barrier = pltpu.get_barrier_semaphore()
    count = jnp.int32(0)
    for dw in (-1, 0, 1):
        for dp in (-1, 0, 1):
            if dp == 0:
                continue
            ok = (w + dw >= 0) & (w + dw < windows) & (p + dp >= 0) & (p + dp < parts)

            @pl.when(ok)
            def _():
                pl.semaphore_signal(
                    barrier, inc=1, device_id={"tm": w + dw, "map": p + dp}, device_id_type=MESH
                )

            count = count + ok.astype(jnp.int32)
    for o in range(1, windows):
        pl.semaphore_signal(
            barrier, inc=1, device_id={"tm": lax.rem(w + o, windows)}, device_id_type=MESH
        )
    count = count + (windows - 1)

    first = p * nb - HALO
    local = [
        [
            [jnp.clip(columns[0, k, j, b] - first, 0, width - 1) for j in range(slots)]
            for b in range(nb)
        ]
        for k in range(2)
    ]
    active = [jnp.full((dirs, tile), steps[0], jnp.int32) > k for k in range(2)]

    def convert(k):
        def row(b, carry):
            load(k, b).wait()
            for j in range(slots):
                x = raw[k, b, j]
                high = x.astype(BF16)
                weights[k, b, :tile, j * tile : (j + 1) * tile] = high
                weights[k, b, tile:, j * tile : (j + 1) * tile] = (
                    x - high.astype(F32)
                ).astype(BF16)
            return carry

        lax.fori_loop(0, nb, row, 0)

    def turn(k):
        def row(b, carry):
            for j in range(slots):
                x = raw[k, b, j].T
                high = x.astype(BF16)
                turned[k, b, j * tile : (j + 1) * tile, :tile] = high
                turned[k, b, j * tile : (j + 1) * tile, tile:] = (
                    x - high.astype(F32)
                ).astype(BF16)
            return carry

        lax.fori_loop(0, nb, row, 0)

    pending = []

    def send(ok, src, dst, send_sem, recv_sem, target):
        copy = pltpu.make_async_remote_copy(
            src_ref=src,
            dst_ref=dst,
            send_sem=send_sem,
            recv_sem=recv_sem,
            device_id=target,
            device_id_type=MESH,
        )

        @pl.when(ok)
        def _():
            copy.start()

        pending.append((ok, copy))

    def arrived(ok, dst, send_sem, recv_sem):
        copy = pltpu.make_async_remote_copy(
            src_ref=dst,
            dst_ref=dst,
            send_sem=send_sem,
            recv_sem=recv_sem,
            device_id={"tm": w, "map": p},
            device_id_type=MESH,
        )

        @pl.when(ok)
        def _():
            copy.wait_recv()

    chunks = ((0, HALO), (nb - HALO, HALO), (HALO, nb - 2 * HALO))
    order = [*range(HALO), *range(nb - HALO, nb), *range(HALO, nb - HALO)]
    low, high_at = slice(0, HALO), slice(HALO, 2 * HALO)

    convert(0)

    @pl.when(has_prev)
    def _():
        convert(1)
        turn(0)
        turn(1)

    for copy in small:
        copy.wait()
    load_rows = [direction[:, b, :] for b in range(nb)]

    def products(k, ext, rows):
        def form(array, contracted):
            for b in rows:
                lhs = jnp.concatenate([ext[local[k][b][j]] for j in range(slots)], axis=1)
                r = lax.dot_general(
                    lhs,
                    array[k, b],
                    (((1,), (contracted,)), ((), ())),
                    preferred_element_type=F32,
                )
                r = r[:dirs] + r[dirs:]
                made[k, b] = r[:, :tile] + r[:, tile:]

        @pl.when(w == 0)
        def _():
            form(weights, 1)

        @pl.when(has_prev)
        def _():
            form(turned, 0)

    for i, (start, size) in enumerate(chunks):
        arrived(has_prev, fin.at[pl.ds(HALO + start, size)], fwd_send.at[i], fwd_recv.at[i])
    arrived(has_prev & has_lo, fin.at[pl.ds(0, HALO)], fwd_send.at[3], fwd_recv.at[3])
    arrived(
        has_prev & has_hi, fin.at[pl.ds(HALO + nb, HALO)], fwd_send.at[4], fwd_recv.at[4]
    )
    for q in range(width):
        ext0[q] = split(fin[q])
    for n, b in enumerate(order):
        if n == 0:
            products(0, ext0, order[: 2 * HALO])
        if n == 2 * HALO:
            products(0, ext0, order[2 * HALO :])
        new = made[0, b] + forcing[0, 0, b : b + 1] * load_rows[b]
        new = jnp.where(active[0], new, fin[HALO + b])
        state1[b] = new
        ext1[HALO + b] = split(new)
        if n == 2 * HALO - 1:
            pl.semaphore_wait(barrier, count)
            send(
                has_lo,
                state1.at[pl.ds(0, HALO)],
                fhalo.at[high_at],
                fh_send.at[0],
                fh_recv.at[0],
                {"tm": w, "map": p - 1},
            )
            send(
                has_hi,
                state1.at[pl.ds(nb - HALO, HALO)],
                fhalo.at[low],
                fh_send.at[1],
                fh_recv.at[1],
                {"tm": w, "map": p + 1},
            )

    @pl.when(w == 0)
    def _():
        convert(1)

    arrived(has_hi, fhalo.at[high_at], fh_send.at[0], fh_recv.at[0])
    arrived(has_lo, fhalo.at[low], fh_send.at[1], fh_recv.at[1])
    for q in range(HALO):
        ext1[q] = split(fhalo[q])
        ext1[HALO + nb + q] = split(fhalo[HALO + q])
    for n, b in enumerate(order):
        if n == 0:
            products(1, ext1, order[: 2 * HALO])
        if n == 2 * HALO:
            products(1, ext1, order[2 * HALO :])
        new = made[1, b] + forcing[0, 1, b : b + 1] * load_rows[b]
        state2[b] = jnp.where(active[1], new, state1[b])
        if n == HALO - 1:
            send(
                has_next & has_lo,
                state2.at[pl.ds(0, HALO)],
                fin.at[pl.ds(HALO + nb, HALO)],
                fwd_send.at[4],
                fwd_recv.at[4],
                {"tm": w + 1, "map": p - 1},
            )
        if n == 2 * HALO - 1:
            send(
                has_next & has_hi,
                state2.at[pl.ds(nb - HALO, HALO)],
                fin.at[pl.ds(0, HALO)],
                fwd_send.at[3],
                fwd_recv.at[3],
                {"tm": w + 1, "map": p + 1},
            )
        for i, (start, size) in enumerate(chunks):
            if n == (HALO - 1, 2 * HALO - 1, nb - 1)[i]:
                send(
                    has_next,
                    state2.at[pl.ds(start, size)],
                    fin.at[pl.ds(HALO + start, size)],
                    fwd_send.at[i],
                    fwd_recv.at[i],
                    {"tm": w + 1, "map": p},
                )

    def scatter(k, b, a, spread):
        s = split(a)
        r = lax.dot_general(
            jnp.concatenate([s, s], axis=1),
            weights[k, b],
            (((1,), (0,)), ((), ())),
            preferred_element_type=F32,
        )
        r = r[:dirs] + r[dirs:]
        for j in range(slots):
            at = jnp.full((dirs, tile), local[k][b][j], jnp.int32)
            part = r[:, j * tile : (j + 1) * tile]
            for q in range(width):
                spread[q] = spread[q] + jnp.where(at == q, part, 0.0)

    seen1 = [observe[0, 1, b : b + 1] * state2[b] for b in range(nb)]
    arrived(has_next, bin_core, bwd_send.at[0], bwd_recv.at[0])
    arrived(has_next & has_lo, bin_rim.at[low], bwd_send.at[1], bwd_recv.at[1])
    arrived(has_next & has_hi, bin_rim.at[high_at], bwd_send.at[2], bwd_recv.at[2])
    carried = [bin_core[b] for b in range(nb)]
    for q in range(HALO):
        carried[q] = carried[q] + bin_rim[q]
        carried[nb - HALO + q] = carried[nb - HALO + q] + bin_rim[HALO + q]
    zero = jnp.zeros((dirs, tile), F32)
    spread = [zero] * width
    gradient = [None] * nb
    for b in range(nb):
        a = carried[b] + seen1[b]
        gradient[b] = jnp.where(active[1], forcing[0, 1, b : b + 1] * a, 0.0)
        scatter(1, b, a, spread)
    for q in range(HALO):
        brim_out[q] = spread[q]
        brim_out[HALO + q] = spread[HALO + nb + q]
    send(
        has_lo,
        brim_out.at[low],
        bhalo.at[high_at],
        bh_send.at[0],
        bh_recv.at[0],
        {"tm": w, "map": p - 1},
    )
    send(
        has_hi,
        brim_out.at[high_at],
        bhalo.at[low],
        bh_send.at[1],
        bh_recv.at[1],
        {"tm": w, "map": p + 1},
    )
    inner = spread[HALO : HALO + nb]
    spread = [zero] * width
    after1 = list(carried)
    for n, b in enumerate([*range(HALO, nb - HALO), *range(HALO), *range(nb - HALO, nb)]):
        if n == nb - 2 * HALO:
            arrived(has_hi, bhalo.at[high_at], bh_send.at[0], bh_recv.at[0])
            arrived(has_lo, bhalo.at[low], bh_send.at[1], bh_recv.at[1])
        value = inner[b]
        if b < HALO:
            value = value + bhalo[b]
        if b >= nb - HALO:
            value = value + bhalo[HALO + b - (nb - HALO)]
        value = jnp.where(active[1], value, carried[b])
        after1[b] = value
        a = value + observe[0, 0, b : b + 1] * state1[b]
        gradient[b] = gradient[b] + jnp.where(
            active[0], forcing[0, 0, b : b + 1] * a, 0.0
        )
        scatter(0, b, a, spread)
    for q in range(HALO):
        brim_out0[q] = jnp.where(active[0], spread[q], 0.0)
        brim_out0[HALO + q] = jnp.where(active[0], spread[HALO + nb + q], 0.0)
    for b in range(nb):
        bcore_out[b] = jnp.where(active[0], spread[HALO + b], after1[b])
    send(
        has_prev & has_lo,
        brim_out0.at[low],
        bin_rim.at[high_at],
        bwd_send.at[2],
        bwd_recv.at[2],
        {"tm": w - 1, "map": p - 1},
    )
    send(
        has_prev & has_hi,
        brim_out0.at[high_at],
        bin_rim.at[low],
        bwd_send.at[1],
        bwd_recv.at[1],
        {"tm": w - 1, "map": p + 1},
    )
    send(
        has_prev,
        bcore_out,
        bin_core,
        bwd_send.at[0],
        bwd_recv.at[0],
        {"tm": w - 1, "map": p},
    )

    for b in range(nb):
        grad_out[:, b, :] = gradient[b]
    always = w >= 0
    for o in range(1, windows):
        target = lax.rem(w + o, windows)
        send(
            always,
            grad_out.at[pl.ds(target * dpw, dpw)],
            grad_in.at[o - 1],
            g_send.at[o - 1],
            g_recv.at[o - 1],
            {"tm": target, "map": p},
        )
    total = grad_out[pl.ds(w * dpw, dpw)]
    for o in range(1, windows):
        arrived(always, grad_in.at[o - 1], g_send.at[o - 1], g_recv.at[o - 1])
        total = total + grad_in[o - 1]
    out[...] = total
    for ok, copy in pending:

        @pl.when(ok)
        def _():
            copy.wait_send()


def shards(windows, parts, tiles, columns, window_steps, direction, forcing, observe):
    dirs, nb, tile = direction.shape
    slots = tiles.shape[3]
    width = nb + 2 * HALO
    dpw = dirs // windows
    vmem = pl.BlockSpec(memory_space=pltpu.VMEM)
    hbm = pl.BlockSpec(memory_space=pltpu.HBM)
    smem = pl.BlockSpec(memory_space=pltpu.SMEM)
    block = lambda *lead: pltpu.VMEM((*lead, dirs, tile), F32)
    sems = lambda n: pltpu.SemaphoreType.DMA((n,))
    return pl.pallas_call(
        functools.partial(kernel, windows, parts),
        out_shape=jax.ShapeDtypeStruct((dpw, nb, tile), F32),
        in_specs=[hbm, smem, smem, hbm, hbm, hbm],
        out_specs=vmem,
        scratch_shapes=[
            pltpu.VMEM(direction.shape, F32),
            pltpu.VMEM(forcing.shape, F32),
            pltpu.VMEM(observe.shape, F32),
            pltpu.VMEM((2, nb, slots, tile, tile), F32),
            pltpu.VMEM((2, nb, 2 * tile, slots * tile), BF16),
            pltpu.VMEM((2, nb, slots * tile, 2 * tile), BF16),
            block(2, nb),
            pltpu.VMEM((width, 2 * dirs, tile), BF16),
            pltpu.VMEM((width, 2 * dirs, tile), BF16),
            block(nb),
            block(nb),
            block(width),
            block(2 * HALO),
            block(nb),
            block(2 * HALO),
            block(2 * HALO),
            block(2 * HALO),
            block(nb),
            block(2 * HALO),
            pltpu.VMEM((dirs, nb, tile), F32),
            pltpu.VMEM((windows - 1, dpw, nb, tile), F32),
            sems(3),
            pltpu.SemaphoreType.DMA((2, nb)),
            sems(5),
            sems(5),
            sems(2),
            sems(2),
            sems(3),
            sems(3),
            sems(2),
            sems(2),
            sems(windows - 1),
            sems(windows - 1),
        ],
        compiler_params=pltpu.CompilerParams(
            collective_id=0, has_side_effects=True, vmem_limit_bytes=63 * 1024 * 1024
        ),
    )(tiles, jnp.swapaxes(columns, 2, 3), window_steps, direction, forcing, observe)


def solution(mesh):
    placed = (
        P("tm", None, "map", None, None, None),
        P("tm", None, "map", None),
        P("tm"),
        P(None, "map", None),
        P("tm", None, "map", None),
        P("tm", None, "map", None),
    )
    return jax.shard_map(
        functools.partial(shards, mesh.shape["tm"], mesh.shape["map"]),
        mesh=mesh,
        in_specs=placed,
        out_specs=P("tm", "map", None),
        check_vma=False,
    )
```

```python
import functools

import jax
import jax.numpy as jnp
from jax import lax
from jax.experimental import pallas as pl
from jax.experimental.pallas import tpu as pltpu
from jax.sharding import PartitionSpec as P

HALO = 2
MESH = pl.DeviceIdType.MESH
F32 = jnp.float32
BF16 = jnp.bfloat16


def split(x):
    high = x.astype(BF16).astype(F32)
    return jnp.concatenate([high, x - high], axis=0).astype(BF16)


def kernel(
    windows,
    parts,
    tiles,
    columns,
    steps,
    direction_far,
    forcing_far,
    observe_far,
    out,
    direction,
    forcing,
    observe,
    raw,
    weights,
    turned,
    made,
    ext0,
    ext1,
    state1,
    state2,
    fin,
    fhalo,
    bin_core,
    bin_rim,
    bhalo,
    brim_out,
    bcore_out,
    brim_out0,
    grad_out,
    grad_in,
    small_sem,
    load_sem,
    fwd_send,
    fwd_recv,
    fh_send,
    fh_recv,
    bwd_send,
    bwd_recv,
    bh_send,
    bh_recv,
    g_send,
    g_recv,
):
    dirs, nb, tile = direction.shape
    slots = columns.shape[2]
    width = nb + 2 * HALO
    dpw = dirs // windows
    w = lax.axis_index("tm")
    p = lax.axis_index("map")
    has_prev, has_next = w > 0, w < windows - 1
    has_lo, has_hi = p > 0, p < parts - 1

    def load(k, b):
        return pltpu.make_async_copy(tiles.at[0, k, b], raw.at[k, b], load_sem.at[k, b])

    for b in range(nb):
        load(0, b).start()
    small = [
        pltpu.make_async_copy(src, dst, small_sem.at[i])
        for i, (src, dst) in enumerate(
            ((direction_far, direction), (forcing_far, forcing), (observe_far, observe))
        )
    ]
    for copy in small:
        copy.start()
    for b in range(nb):
        load(1, b).start()
    for ref in (fin, fhalo, bin_core, bin_rim, bhalo):
        ref[...] = jnp.zeros(ref.shape, F32)

    barrier = pltpu.get_barrier_semaphore()
    count = jnp.int32(0)
    for dw in (-1, 0, 1):
        for dp in (-1, 0, 1):
            if dp == 0:
                continue
            ok = (w + dw >= 0) & (w + dw < windows) & (p + dp >= 0) & (p + dp < parts)

            @pl.when(ok)
            def _():
                pl.semaphore_signal(
                    barrier, inc=1, device_id={"tm": w + dw, "map": p + dp}, device_id_type=MESH
                )

            count = count + ok.astype(jnp.int32)
    for o in range(1, windows):
        pl.semaphore_signal(
            barrier, inc=1, device_id={"tm": lax.rem(w + o, windows)}, device_id_type=MESH
        )
    count = count + (windows - 1)

    first = p * nb - HALO
    local = [
        [
            [jnp.clip(columns[0, k, j, b] - first, 0, width - 1) for j in range(slots)]
            for b in range(nb)
        ]
        for k in range(2)
    ]
    active = [jnp.full((dirs, tile), steps[0], jnp.int32) > k for k in range(2)]

    def convert(k):
        def row(b, carry):
            load(k, b).wait()
            for j in range(slots):
                x = raw[k, b, j]
                high = x.astype(BF16)
                weights[k, b, :tile, j * tile : (j + 1) * tile] = high
                weights[k, b, tile:, j * tile : (j + 1) * tile] = (
                    x - high.astype(F32)
                ).astype(BF16)
            return carry

        lax.fori_loop(0, nb, row, 0)

    def turn(k):
        def row(b, carry):
            for j in range(slots):
                x = raw[k, b, j].T
                high = x.astype(BF16)
                turned[k, b, j * tile : (j + 1) * tile, :tile] = high
                turned[k, b, j * tile : (j + 1) * tile, tile:] = (
                    x - high.astype(F32)
                ).astype(BF16)
            return carry

        lax.fori_loop(0, nb, row, 0)

    pending = []

    def send(ok, src, dst, send_sem, recv_sem, target):
        copy = pltpu.make_async_remote_copy(
            src_ref=src,
            dst_ref=dst,
            send_sem=send_sem,
            recv_sem=recv_sem,
            device_id=target,
            device_id_type=MESH,
        )

        @pl.when(ok)
        def _():
            copy.start()

        pending.append((ok, copy))

    def arrived(ok, dst, send_sem, recv_sem):
        copy = pltpu.make_async_remote_copy(
            src_ref=dst,
            dst_ref=dst,
            send_sem=send_sem,
            recv_sem=recv_sem,
            device_id={"tm": w, "map": p},
            device_id_type=MESH,
        )

        @pl.when(ok)
        def _():
            copy.wait_recv()

    chunks = ((0, HALO), (nb - HALO, HALO), (HALO, nb - 2 * HALO))
    order = [*range(HALO), *range(nb - HALO, nb), *range(HALO, nb - HALO)]
    low, high_at = slice(0, HALO), slice(HALO, 2 * HALO)

    convert(0)

    @pl.when(has_prev)
    def _():
        convert(1)
        turn(0)
        turn(1)

    for copy in small:
        copy.wait()
    load_rows = [direction[:, b, :] for b in range(nb)]

    def products(k, ext, rows):
        def form(array, contracted):
            for b in rows:
                lhs = jnp.concatenate([ext[local[k][b][j]] for j in range(slots)], axis=1)
                r = lax.dot_general(
                    lhs,
                    array[k, b],
                    (((1,), (contracted,)), ((), ())),
                    preferred_element_type=F32,
                )
                r = r[:dirs] + r[dirs:]
                made[k, b] = r[:, :tile] + r[:, tile:]

        @pl.when(w == 0)
        def _():
            form(weights, 1)

        @pl.when(has_prev)
        def _():
            form(turned, 0)

    for i, (start, size) in enumerate(chunks):
        arrived(has_prev, fin.at[pl.ds(HALO + start, size)], fwd_send.at[i], fwd_recv.at[i])
    arrived(has_prev & has_lo, fin.at[pl.ds(0, HALO)], fwd_send.at[3], fwd_recv.at[3])
    arrived(
        has_prev & has_hi, fin.at[pl.ds(HALO + nb, HALO)], fwd_send.at[4], fwd_recv.at[4]
    )
    for q in range(width):
        ext0[q] = split(fin[q])
    for n, b in enumerate(order):
        if n == 0:
            products(0, ext0, order[: 2 * HALO])
        if n == 2 * HALO:
            products(0, ext0, order[2 * HALO :])
        new = made[0, b] + forcing[0, 0, b : b + 1] * load_rows[b]
        new = jnp.where(active[0], new, fin[HALO + b])
        state1[b] = new
        ext1[HALO + b] = split(new)
        if n == 2 * HALO - 1:
            pl.semaphore_wait(barrier, count)
            send(
                has_lo,
                state1.at[pl.ds(0, HALO)],
                fhalo.at[high_at],
                fh_send.at[0],
                fh_recv.at[0],
                {"tm": w, "map": p - 1},
            )
            send(
                has_hi,
                state1.at[pl.ds(nb - HALO, HALO)],
                fhalo.at[low],
                fh_send.at[1],
                fh_recv.at[1],
                {"tm": w, "map": p + 1},
            )

    @pl.when(w == 0)
    def _():
        convert(1)

    arrived(has_hi, fhalo.at[high_at], fh_send.at[0], fh_recv.at[0])
    arrived(has_lo, fhalo.at[low], fh_send.at[1], fh_recv.at[1])
    for q in range(HALO):
        ext1[q] = split(fhalo[q])
        ext1[HALO + nb + q] = split(fhalo[HALO + q])
    for n, b in enumerate(order):
        if n == 0:
            products(1, ext1, order[: 2 * HALO])
        if n == 2 * HALO:
            products(1, ext1, order[2 * HALO :])
        new = made[1, b] + forcing[0, 1, b : b + 1] * load_rows[b]
        state2[b] = jnp.where(active[1], new, state1[b])
        if n == HALO - 1:
            send(
                has_next & has_lo,
                state2.at[pl.ds(0, HALO)],
                fin.at[pl.ds(HALO + nb, HALO)],
                fwd_send.at[4],
                fwd_recv.at[4],
                {"tm": w + 1, "map": p - 1},
            )
        if n == 2 * HALO - 1:
            send(
                has_next & has_hi,
                state2.at[pl.ds(nb - HALO, HALO)],
                fin.at[pl.ds(0, HALO)],
                fwd_send.at[3],
                fwd_recv.at[3],
                {"tm": w + 1, "map": p + 1},
            )
        for i, (start, size) in enumerate(chunks):
            if n == (HALO - 1, 2 * HALO - 1, nb - 1)[i]:
                send(
                    has_next,
                    state2.at[pl.ds(start, size)],
                    fin.at[pl.ds(HALO + start, size)],
                    fwd_send.at[i],
                    fwd_recv.at[i],
                    {"tm": w + 1, "map": p},
                )

    def scatter(k, b, a, spread):
        s = split(a)
        r = lax.dot_general(
            jnp.concatenate([s, s], axis=1),
            weights[k, b],
            (((1,), (0,)), ((), ())),
            preferred_element_type=F32,
        )
        r = r[:dirs] + r[dirs:]
        for j in range(slots):
            at = jnp.full((dirs, tile), local[k][b][j], jnp.int32)
            part = r[:, j * tile : (j + 1) * tile]
            for q in range(width):
                spread[q] = spread[q] + jnp.where(at == q, part, 0.0)

    seen1 = [observe[0, 1, b : b + 1] * state2[b] for b in range(nb)]
    arrived(has_next, bin_core, bwd_send.at[0], bwd_recv.at[0])
    arrived(has_next & has_lo, bin_rim.at[low], bwd_send.at[1], bwd_recv.at[1])
    arrived(has_next & has_hi, bin_rim.at[high_at], bwd_send.at[2], bwd_recv.at[2])
    carried = [bin_core[b] for b in range(nb)]
    for q in range(HALO):
        carried[q] = carried[q] + bin_rim[q]
        carried[nb - HALO + q] = carried[nb - HALO + q] + bin_rim[HALO + q]
    zero = jnp.zeros((dirs, tile), F32)
    spread = [zero] * width
    gradient = [None] * nb
    for b in range(nb):
        a = carried[b] + seen1[b]
        gradient[b] = jnp.where(active[1], forcing[0, 1, b : b + 1] * a, 0.0)
        scatter(1, b, a, spread)
    for q in range(HALO):
        brim_out[q] = spread[q]
        brim_out[HALO + q] = spread[HALO + nb + q]
    send(
        has_lo,
        brim_out.at[low],
        bhalo.at[high_at],
        bh_send.at[0],
        bh_recv.at[0],
        {"tm": w, "map": p - 1},
    )
    send(
        has_hi,
        brim_out.at[high_at],
        bhalo.at[low],
        bh_send.at[1],
        bh_recv.at[1],
        {"tm": w, "map": p + 1},
    )
    inner = spread[HALO : HALO + nb]
    def last_step(handed_on):
        spread = [zero] * width
        after1 = list(carried)
        terms = list(gradient)
        for n, b in enumerate([*range(HALO, nb - HALO), *range(HALO), *range(nb - HALO, nb)]):
            if n == nb - 2 * HALO:
                arrived(has_hi, bhalo.at[high_at], bh_send.at[0], bh_recv.at[0])
                arrived(has_lo, bhalo.at[low], bh_send.at[1], bh_recv.at[1])
            value = inner[b]
            if b < HALO:
                value = value + bhalo[b]
            if b >= nb - HALO:
                value = value + bhalo[HALO + b - (nb - HALO)]
            value = jnp.where(active[1], value, carried[b])
            after1[b] = value
            a = value + observe[0, 0, b : b + 1] * state1[b]
            terms[b] = terms[b] + jnp.where(
                active[0], forcing[0, 0, b : b + 1] * a, 0.0
            )
            if handed_on:
                scatter(0, b, a, spread)
        if handed_on:
            for q in range(HALO):
                brim_out0[q] = jnp.where(active[0], spread[q], 0.0)
                brim_out0[HALO + q] = jnp.where(active[0], spread[HALO + nb + q], 0.0)
            for b in range(nb):
                bcore_out[b] = jnp.where(active[0], spread[HALO + b], after1[b])
        for b in range(nb):
            grad_out[:, b, :] = terms[b]

    @pl.when(w == 0)
    def _():
        last_step(False)

    @pl.when(has_prev)
    def _():
        last_step(True)

    send(
        has_prev & has_lo,
        brim_out0.at[low],
        bin_rim.at[high_at],
        bwd_send.at[2],
        bwd_recv.at[2],
        {"tm": w - 1, "map": p - 1},
    )
    send(
        has_prev & has_hi,
        brim_out0.at[high_at],
        bin_rim.at[low],
        bwd_send.at[1],
        bwd_recv.at[1],
        {"tm": w - 1, "map": p + 1},
    )
    send(
        has_prev,
        bcore_out,
        bin_core,
        bwd_send.at[0],
        bwd_recv.at[0],
        {"tm": w - 1, "map": p},
    )

    always = w >= 0
    for o in range(1, windows):
        target = lax.rem(w + o, windows)
        send(
            always,
            grad_out.at[pl.ds(target * dpw, dpw)],
            grad_in.at[o - 1],
            g_send.at[o - 1],
            g_recv.at[o - 1],
            {"tm": target, "map": p},
        )
    total = grad_out[pl.ds(w * dpw, dpw)]
    for o in range(1, windows):
        arrived(always, grad_in.at[o - 1], g_send.at[o - 1], g_recv.at[o - 1])
        total = total + grad_in[o - 1]
    out[...] = total
    for ok, copy in pending:

        @pl.when(ok)
        def _():
            copy.wait_send()


def shards(windows, parts, tiles, columns, window_steps, direction, forcing, observe):
    dirs, nb, tile = direction.shape
    slots = tiles.shape[3]
    width = nb + 2 * HALO
    dpw = dirs // windows
    vmem = pl.BlockSpec(memory_space=pltpu.VMEM)
    hbm = pl.BlockSpec(memory_space=pltpu.HBM)
    smem = pl.BlockSpec(memory_space=pltpu.SMEM)
    block = lambda *lead: pltpu.VMEM((*lead, dirs, tile), F32)
    sems = lambda n: pltpu.SemaphoreType.DMA((n,))
    return pl.pallas_call(
        functools.partial(kernel, windows, parts),
        out_shape=jax.ShapeDtypeStruct((dpw, nb, tile), F32),
        in_specs=[hbm, smem, smem, hbm, hbm, hbm],
        out_specs=vmem,
        scratch_shapes=[
            pltpu.VMEM(direction.shape, F32),
            pltpu.VMEM(forcing.shape, F32),
            pltpu.VMEM(observe.shape, F32),
            pltpu.VMEM((2, nb, slots, tile, tile), F32),
            pltpu.VMEM((2, nb, 2 * tile, slots * tile), BF16),
            pltpu.VMEM((2, nb, slots * tile, 2 * tile), BF16),
            block(2, nb),
            pltpu.VMEM((width, 2 * dirs, tile), BF16),
            pltpu.VMEM((width, 2 * dirs, tile), BF16),
            block(nb),
            block(nb),
            block(width),
            block(2 * HALO),
            block(nb),
            block(2 * HALO),
            block(2 * HALO),
            block(2 * HALO),
            block(nb),
            block(2 * HALO),
            pltpu.VMEM((dirs, nb, tile), F32),
            pltpu.VMEM((windows - 1, dpw, nb, tile), F32),
            sems(3),
            pltpu.SemaphoreType.DMA((2, nb)),
            sems(5),
            sems(5),
            sems(2),
            sems(2),
            sems(3),
            sems(3),
            sems(2),
            sems(2),
            sems(windows - 1),
            sems(windows - 1),
        ],
        compiler_params=pltpu.CompilerParams(
            collective_id=0, has_side_effects=True, vmem_limit_bytes=63 * 1024 * 1024
        ),
    )(tiles, jnp.swapaxes(columns, 2, 3), window_steps, direction, forcing, observe)


def solution(mesh):
    placed = (
        P("tm", None, "map", None, None, None),
        P("tm", None, "map", None),
        P("tm"),
        P(None, "map", None),
        P("tm", None, "map", None),
        P("tm", None, "map", None),
    )
    return jax.shard_map(
        functools.partial(shards, mesh.shape["tm"], mesh.shape["map"]),
        mesh=mesh,
        in_specs=placed,
        out_specs=P("tm", "map", None),
        check_vma=False,
    )
```

```python
import functools

import jax
import jax.numpy as jnp
from jax import lax
from jax.experimental import pallas as pl
from jax.experimental.pallas import tpu as pltpu
from jax.sharding import PartitionSpec as P

HALO = 2
MESH = pl.DeviceIdType.MESH
F32 = jnp.float32
BF16 = jnp.bfloat16


def split(x):
    high = x.astype(BF16).astype(F32)
    return jnp.concatenate([high, x - high], axis=0).astype(BF16)


def kernel(
    windows,
    parts,
    tiles,
    columns,
    steps,
    direction_far,
    forcing_far,
    observe_far,
    out,
    direction,
    forcing,
    observe,
    raw,
    weights,
    turned,
    made,
    ext0,
    ext1,
    state1,
    state2,
    fin,
    fhalo,
    bin_core,
    bin_rim,
    bhalo,
    brim_out,
    bcore_out,
    brim_out0,
    grad_out,
    grad_in,
    small_sem,
    load_sem,
    fwd_send,
    fwd_recv,
    fh_send,
    fh_recv,
    bwd_send,
    bwd_recv,
    bh_send,
    bh_recv,
    g_send,
    g_recv,
):
    dirs, nb, tile = direction.shape
    slots = columns.shape[2]
    width = nb + 2 * HALO
    dpw = dirs // windows
    w = lax.axis_index("tm")
    p = lax.axis_index("map")
    has_prev, has_next = w > 0, w < windows - 1
    has_lo, has_hi = p > 0, p < parts - 1

    def load(k, b):
        return pltpu.make_async_copy(tiles.at[0, k, b], raw.at[k, b], load_sem.at[k, b])

    for b in range(nb):
        load(0, b).start()
    small = [
        pltpu.make_async_copy(src, dst, small_sem.at[i])
        for i, (src, dst) in enumerate(
            ((direction_far, direction), (forcing_far, forcing), (observe_far, observe))
        )
    ]
    for copy in small:
        copy.start()
    for b in range(nb):
        load(1, b).start()
    for ref in (fin, fhalo, bin_core, bin_rim, bhalo):
        ref[...] = jnp.zeros(ref.shape, F32)

    barrier = pltpu.get_barrier_semaphore()
    count = jnp.int32(0)
    for dw in (-1, 0, 1):
        for dp in (-1, 0, 1):
            if dp == 0:
                continue
            ok = (w + dw >= 0) & (w + dw < windows) & (p + dp >= 0) & (p + dp < parts)

            @pl.when(ok)
            def _():
                pl.semaphore_signal(
                    barrier, inc=1, device_id={"tm": w + dw, "map": p + dp}, device_id_type=MESH
                )

            count = count + ok.astype(jnp.int32)
    for o in range(1, windows):
        pl.semaphore_signal(
            barrier, inc=1, device_id={"tm": lax.rem(w + o, windows)}, device_id_type=MESH
        )
    count = count + (windows - 1)

    first = p * nb - HALO
    local = [
        [
            [jnp.clip(columns[0, k, j, b] - first, 0, width - 1) for j in range(slots)]
            for b in range(nb)
        ]
        for k in range(2)
    ]
    active = [jnp.full((dirs, tile), steps[0], jnp.int32) > k for k in range(2)]

    def convert(k):
        def row(b, carry):
            load(k, b).wait()
            for j in range(slots):
                x = raw[k, b, j]
                high = x.astype(BF16)
                weights[k, b, :tile, j * tile : (j + 1) * tile] = high
                weights[k, b, tile:, j * tile : (j + 1) * tile] = (
                    x - high.astype(F32)
                ).astype(BF16)
            return carry

        lax.fori_loop(0, nb, row, 0)

    def turn(k):
        def row(b, carry):
            for j in range(slots):
                x = raw[k, b, j].T
                high = x.astype(BF16)
                turned[k, b, j * tile : (j + 1) * tile, :tile] = high
                turned[k, b, j * tile : (j + 1) * tile, tile:] = (
                    x - high.astype(F32)
                ).astype(BF16)
            return carry

        lax.fori_loop(0, nb, row, 0)

    pending = []

    def send(ok, src, dst, send_sem, recv_sem, target):
        copy = pltpu.make_async_remote_copy(
            src_ref=src,
            dst_ref=dst,
            send_sem=send_sem,
            recv_sem=recv_sem,
            device_id=target,
            device_id_type=MESH,
        )

        @pl.when(ok)
        def _():
            copy.start()

        pending.append((ok, copy))

    def arrived(ok, dst, send_sem, recv_sem):
        copy = pltpu.make_async_remote_copy(
            src_ref=dst,
            dst_ref=dst,
            send_sem=send_sem,
            recv_sem=recv_sem,
            device_id={"tm": w, "map": p},
            device_id_type=MESH,
        )

        @pl.when(ok)
        def _():
            copy.wait_recv()

    chunks = ((0, HALO), (nb - HALO, HALO), (HALO, nb - 2 * HALO))
    order = [*range(HALO), *range(nb - HALO, nb), *range(HALO, nb - HALO)]
    low, high_at = slice(0, HALO), slice(HALO, 2 * HALO)

    convert(0)

    @pl.when(has_prev)
    def _():
        convert(1)
        turn(0)
        turn(1)

    for copy in small:
        copy.wait()
    load_rows = [direction[:, b, :] for b in range(nb)]

    def products(k, ext, rows):
        def form(array, contracted):
            for b in rows:
                lhs = jnp.concatenate([ext[local[k][b][j]] for j in range(slots)], axis=1)
                r = lax.dot_general(
                    lhs,
                    array[k, b],
                    (((1,), (contracted,)), ((), ())),
                    preferred_element_type=F32,
                )
                r = r[:dirs] + r[dirs:]
                made[k, b] = r[:, :tile] + r[:, tile:]

        @pl.when(w == 0)
        def _():
            form(weights, 1)

        @pl.when(has_prev)
        def _():
            form(turned, 0)

    for i, (start, size) in enumerate(chunks):
        arrived(has_prev, fin.at[pl.ds(HALO + start, size)], fwd_send.at[i], fwd_recv.at[i])
    arrived(has_prev & has_lo, fin.at[pl.ds(0, HALO)], fwd_send.at[3], fwd_recv.at[3])
    arrived(
        has_prev & has_hi, fin.at[pl.ds(HALO + nb, HALO)], fwd_send.at[4], fwd_recv.at[4]
    )
    for q in range(width):
        ext0[q] = split(fin[q])
    for n, b in enumerate(order):
        if n == 0:
            products(0, ext0, order[: 2 * HALO])
        if n == 2 * HALO:
            products(0, ext0, order[2 * HALO :])
        new = made[0, b] + forcing[0, 0, b : b + 1] * load_rows[b]
        new = jnp.where(active[0], new, fin[HALO + b])
        state1[b] = new
        ext1[HALO + b] = split(new)
        if n == 2 * HALO - 1:
            pl.semaphore_wait(barrier, count)
            send(
                has_lo,
                state1.at[pl.ds(0, HALO)],
                fhalo.at[high_at],
                fh_send.at[0],
                fh_recv.at[0],
                {"tm": w, "map": p - 1},
            )
            send(
                has_hi,
                state1.at[pl.ds(nb - HALO, HALO)],
                fhalo.at[low],
                fh_send.at[1],
                fh_recv.at[1],
                {"tm": w, "map": p + 1},
            )

    @pl.when(w == 0)
    def _():
        convert(1)

    arrived(has_hi, fhalo.at[high_at], fh_send.at[0], fh_recv.at[0])
    arrived(has_lo, fhalo.at[low], fh_send.at[1], fh_recv.at[1])
    for q in range(HALO):
        ext1[q] = split(fhalo[q])
        ext1[HALO + nb + q] = split(fhalo[HALO + q])
    for n, b in enumerate(order):
        if n == 0:
            products(1, ext1, order[: 2 * HALO])
        if n == 2 * HALO:
            products(1, ext1, order[2 * HALO :])
        new = made[1, b] + forcing[0, 1, b : b + 1] * load_rows[b]
        state2[b] = jnp.where(active[1], new, state1[b])
        if n == HALO - 1:
            send(
                has_next & has_lo,
                state2.at[pl.ds(0, HALO)],
                fin.at[pl.ds(HALO + nb, HALO)],
                fwd_send.at[4],
                fwd_recv.at[4],
                {"tm": w + 1, "map": p - 1},
            )
        if n == 2 * HALO - 1:
            send(
                has_next & has_hi,
                state2.at[pl.ds(nb - HALO, HALO)],
                fin.at[pl.ds(0, HALO)],
                fwd_send.at[3],
                fwd_recv.at[3],
                {"tm": w + 1, "map": p + 1},
            )
        for i, (start, size) in enumerate(chunks):
            if n == (HALO - 1, 2 * HALO - 1, nb - 1)[i]:
                send(
                    has_next,
                    state2.at[pl.ds(start, size)],
                    fin.at[pl.ds(HALO + start, size)],
                    fwd_send.at[i],
                    fwd_recv.at[i],
                    {"tm": w + 1, "map": p},
                )

    held = []
    rim = [*range(HALO), *range(HALO + nb, width)]
    core = range(HALO, HALO + nb)

    def scatter(k, b, a, spread):
        s = split(a)
        r = lax.dot_general(
            jnp.concatenate([s, s], axis=1),
            weights[k, b],
            (((1,), (0,)), ((), ())),
            preferred_element_type=F32,
        )
        r = r[:dirs] + r[dirs:]
        held.append((k, b, r))

    def rims_then_inner(spread, wanted):
        for k, b, r in held:
            for j in range(slots):
                at = jnp.full((dirs, tile), local[k][b][j], jnp.int32)
                part = r[:, j * tile : (j + 1) * tile]
                for q in wanted:
                    spread[q] = spread[q] + jnp.where(at == q, part, 0.0)

    seen1 = [observe[0, 1, b : b + 1] * state2[b] for b in range(nb)]
    arrived(has_next, bin_core, bwd_send.at[0], bwd_recv.at[0])
    arrived(has_next & has_lo, bin_rim.at[low], bwd_send.at[1], bwd_recv.at[1])
    arrived(has_next & has_hi, bin_rim.at[high_at], bwd_send.at[2], bwd_recv.at[2])
    carried = [bin_core[b] for b in range(nb)]
    for q in range(HALO):
        carried[q] = carried[q] + bin_rim[q]
        carried[nb - HALO + q] = carried[nb - HALO + q] + bin_rim[HALO + q]
    zero = jnp.zeros((dirs, tile), F32)
    spread = [zero] * width
    gradient = [None] * nb
    for b in range(nb):
        a = carried[b] + seen1[b]
        gradient[b] = jnp.where(active[1], forcing[0, 1, b : b + 1] * a, 0.0)
        scatter(1, b, a, spread)
    rims_then_inner(spread, rim)
    for q in range(HALO):
        brim_out[q] = spread[q]
        brim_out[HALO + q] = spread[HALO + nb + q]
    send(
        has_lo,
        brim_out.at[low],
        bhalo.at[high_at],
        bh_send.at[0],
        bh_recv.at[0],
        {"tm": w, "map": p - 1},
    )
    send(
        has_hi,
        brim_out.at[high_at],
        bhalo.at[low],
        bh_send.at[1],
        bh_recv.at[1],
        {"tm": w, "map": p + 1},
    )
    rims_then_inner(spread, core)
    held.clear()
    inner = spread[HALO : HALO + nb]
    spread = [zero] * width
    after1 = list(carried)
    for n, b in enumerate([*range(HALO, nb - HALO), *range(HALO), *range(nb - HALO, nb)]):
        if n == nb - 2 * HALO:
            arrived(has_hi, bhalo.at[high_at], bh_send.at[0], bh_recv.at[0])
            arrived(has_lo, bhalo.at[low], bh_send.at[1], bh_recv.at[1])
        value = inner[b]
        if b < HALO:
            value = value + bhalo[b]
        if b >= nb - HALO:
            value = value + bhalo[HALO + b - (nb - HALO)]
        value = jnp.where(active[1], value, carried[b])
        after1[b] = value
        a = value + observe[0, 0, b : b + 1] * state1[b]
        gradient[b] = gradient[b] + jnp.where(
            active[0], forcing[0, 0, b : b + 1] * a, 0.0
        )
        scatter(0, b, a, spread)
    rims_then_inner(spread, rim)
    for q in range(HALO):
        brim_out0[q] = jnp.where(active[0], spread[q], 0.0)
        brim_out0[HALO + q] = jnp.where(active[0], spread[HALO + nb + q], 0.0)
    send(
        has_prev & has_lo,
        brim_out0.at[low],
        bin_rim.at[high_at],
        bwd_send.at[2],
        bwd_recv.at[2],
        {"tm": w - 1, "map": p - 1},
    )
    send(
        has_prev & has_hi,
        brim_out0.at[high_at],
        bin_rim.at[low],
        bwd_send.at[1],
        bwd_recv.at[1],
        {"tm": w - 1, "map": p + 1},
    )
    rims_then_inner(spread, core)
    for b in range(nb):
        bcore_out[b] = jnp.where(active[0], spread[HALO + b], after1[b])
    send(
        has_prev,
        bcore_out,
        bin_core,
        bwd_send.at[0],
        bwd_recv.at[0],
        {"tm": w - 1, "map": p},
    )

    for b in range(nb):
        grad_out[:, b, :] = gradient[b]
    always = w >= 0
    for o in range(1, windows):
        target = lax.rem(w + o, windows)
        send(
            always,
            grad_out.at[pl.ds(target * dpw, dpw)],
            grad_in.at[o - 1],
            g_send.at[o - 1],
            g_recv.at[o - 1],
            {"tm": target, "map": p},
        )
    total = grad_out[pl.ds(w * dpw, dpw)]
    for o in range(1, windows):
        arrived(always, grad_in.at[o - 1], g_send.at[o - 1], g_recv.at[o - 1])
        total = total + grad_in[o - 1]
    out[...] = total
    for ok, copy in pending:

        @pl.when(ok)
        def _():
            copy.wait_send()


def shards(windows, parts, tiles, columns, window_steps, direction, forcing, observe):
    dirs, nb, tile = direction.shape
    slots = tiles.shape[3]
    width = nb + 2 * HALO
    dpw = dirs // windows
    vmem = pl.BlockSpec(memory_space=pltpu.VMEM)
    hbm = pl.BlockSpec(memory_space=pltpu.HBM)
    smem = pl.BlockSpec(memory_space=pltpu.SMEM)
    block = lambda *lead: pltpu.VMEM((*lead, dirs, tile), F32)
    sems = lambda n: pltpu.SemaphoreType.DMA((n,))
    return pl.pallas_call(
        functools.partial(kernel, windows, parts),
        out_shape=jax.ShapeDtypeStruct((dpw, nb, tile), F32),
        in_specs=[hbm, smem, smem, hbm, hbm, hbm],
        out_specs=vmem,
        scratch_shapes=[
            pltpu.VMEM(direction.shape, F32),
            pltpu.VMEM(forcing.shape, F32),
            pltpu.VMEM(observe.shape, F32),
            pltpu.VMEM((2, nb, slots, tile, tile), F32),
            pltpu.VMEM((2, nb, 2 * tile, slots * tile), BF16),
            pltpu.VMEM((2, nb, slots * tile, 2 * tile), BF16),
            block(2, nb),
            pltpu.VMEM((width, 2 * dirs, tile), BF16),
            pltpu.VMEM((width, 2 * dirs, tile), BF16),
            block(nb),
            block(nb),
            block(width),
            block(2 * HALO),
            block(nb),
            block(2 * HALO),
            block(2 * HALO),
            block(2 * HALO),
            block(nb),
            block(2 * HALO),
            pltpu.VMEM((dirs, nb, tile), F32),
            pltpu.VMEM((windows - 1, dpw, nb, tile), F32),
            sems(3),
            pltpu.SemaphoreType.DMA((2, nb)),
            sems(5),
            sems(5),
            sems(2),
            sems(2),
            sems(3),
            sems(3),
            sems(2),
            sems(2),
            sems(windows - 1),
            sems(windows - 1),
        ],
        compiler_params=pltpu.CompilerParams(
            collective_id=0, has_side_effects=True, vmem_limit_bytes=63 * 1024 * 1024
        ),
    )(tiles, jnp.swapaxes(columns, 2, 3), window_steps, direction, forcing, observe)


def solution(mesh):
    placed = (
        P("tm", None, "map", None, None, None),
        P("tm", None, "map", None),
        P("tm"),
        P(None, "map", None),
        P("tm", None, "map", None),
        P("tm", None, "map", None),
    )
    return jax.shard_map(
        functools.partial(shards, mesh.shape["tm"], mesh.shape["map"]),
        mesh=mesh,
        in_specs=placed,
        out_specs=P("tm", "map", None),
        check_vma=False,
    )
```
